32 devices in a mesh: row: 16 (over z, y, x), col: 2 (over core).
Axes of the slice: x: 2, y: 2, z: 4, core: 2. Of those that a mesh axis runs over, the one named last changes fastest.
Arguments:
- top_inverse: float32 [2, 1024, 1024], P(None, 'row', 'col'), may hold values from -6 to 6, as said below
- blocks_upper: int32 [2, 2], replicated, may hold values from 0 to 3, as said below
- factor_upper: float32 [2, 2, 512, 4096], P(None, None, 'row', 'col'), may hold values from -0.1875 to 0.1875
- diagonal_upper: float32 [2, 2, 4096, 4096], P(None, None, 'row', 'col'), may hold values from -6 to 6, as said below
- parents_lower: int32 [3], replicated, may hold values from 0 to 1
- blocks_lower: int32 [3, 2], replicated, may hold values from 0 to 15, as said below
- factor_lower: float32 [3, 2, 512, 4096], P(None, None, 'row', 'col'), may hold values from -0.1875 to 0.1875
- diagonal_lower: float32 [3, 2, 4096, 4096], P(None, None, 'row', 'col'), may hold values from -6 to 6, as said below
Outputs:
- coupling_inverse_upper: float32 [2, 2, 4096, 512], P(None, None, 'row')
- block_inverse_upper: float32 [2, 2, 4096, 4096], P(None, None, 'row', 'col')
- coupling_inverse_lower: float32 [3, 2, 4096, 512], P(None, None, 'row')
- block_inverse_lower: float32 [3, 2, 4096, 4096], P(None, None, 'row', 'col')
The draws below stay inside these ranges and needn't reach their ends.
Inputs may be any that keep to these rules, and one draw needn't show every extreme that they name: `top_inverse`: equal to its own transpose (no conjugation) in both parts. `diagonal_upper`: each matrix equals its own transpose (no conjugation) in both parts. `diagonal_lower`: each matrix equals its own transpose (no conjugation) in both parts. `blocks_upper`: each row names 2 different blocks. `blocks_lower`: each row names 2 different blocks.
All inputs are finite; a program needn't handle non-finite values.
Results may differ from the reference program's by a relative error of at most 0.00011.
Values sent between devices are 32-bit elements; how exact they have to be, the bound alone decides.
A program may use at most 256 MiB of HBM per device.

```python
import jax
import jax.numpy as jnp
from jax import lax

BS = 256
W = 4096
KB = 16
NB = 2
CS = 512
NTB = 4
NT = 1024
UPPER = 2
LOWER = 3


def symmetric_draw(key, number, side_length):
    extent = (number, 2, side_length, side_length)
    values = jax.random.normal(key, extent, jnp.float32)
    values = (values + jnp.swapaxes(values, 2, 3)) * 0.7071
    return jnp.clip(values, -6.0, 6.0)


def block_lists(key, number, blocks_total):
    inner = 1 + jax.random.permutation(jax.random.fold_in(key, 0), max(blocks_total - 2, 1))[:NB - 2]
    leading = jnp.concatenate([jnp.array([0, blocks_total - 1], jnp.int32), inner.astype(jnp.int32)])
    leading = leading[jax.random.permutation(jax.random.fold_in(key, 1), NB)]
    rows_all = [leading]
    for sibling in range(1, number):
        picked = jax.random.permutation(jax.random.fold_in(key, sibling + 2), blocks_total)[:NB]
        rows_all.append(picked.astype(jnp.int32))
    return jnp.stack(rows_all)


def draw_top_inverse(key, part):
    return symmetric_draw(jax.random.fold_in(key, 11), 1, NT)[0]


def draw_diagonal_upper(key, part):
    return symmetric_draw(jax.random.fold_in(key, 12), UPPER, W)


def draw_diagonal_lower(key, part):
    return symmetric_draw(jax.random.fold_in(key, 13), LOWER, W)


def draw_blocks_upper(key, part):
    return block_lists(jax.random.fold_in(key, 14), UPPER, NTB)


def draw_blocks_lower(key, part):
    return block_lists(jax.random.fold_in(key, 15), LOWER, KB)


def draw_parents_lower(key, part):
    base_key = jax.random.fold_in(key, 16)
    leading = jax.random.permutation(jax.random.fold_in(base_key, 0), UPPER).astype(jnp.int32)
    others = jax.random.randint(jax.random.fold_in(base_key, 1), (LOWER - UPPER,), 0, UPPER).astype(jnp.int32)
    joined = jnp.concatenate([leading, others])
    return joined[jax.random.permutation(jax.random.fold_in(base_key, 2), LOWER)]


def levels(key, shape, shards, least, top_value):
    def one(dim, shards_of):
        steps = jax.random.uniform(jax.random.fold_in(jax.random.fold_in(key, 6), dim), (shards_of,), jnp.float32, least / len(shards), top_value / len(shards))
        return jnp.repeat(jnp.exp(steps), shape[dim] // shards_of).reshape((-1,) + (1,) * (len(shape) - dim - 1))

    factor_of = one(*shards[0])
    for cut in shards[1:]:
        factor_of = factor_of * one(*cut)
    return factor_of


def normal_values(stream_key, shape, scale, limit, cuts=(), kind=jnp.bfloat16):
    level = levels(stream_key, shape, cuts, -0.22, 0.18) if cuts else 1.0
    drawn = jax.random.normal(stream_key, shape, jnp.float32) * scale * level
    return jnp.minimum(jnp.maximum(drawn, -limit), limit).astype(kind)


def setup_inputs(seed: int = 0) -> dict:
    splits = jax.random.split(jax.random.key(seed), 9)
    top_inverse = draw_top_inverse(jax.random.fold_in(splits[8], 71), 0)
    blocks_upper = draw_blocks_upper(jax.random.fold_in(splits[8], 71), 0)
    factor_upper = normal_values(splits[2], (UPPER, 2, CS, W), (2 * CS) ** -0.5, 0.1875, ((2, 16), (3, 2)), jnp.float32)
    diagonal_upper = draw_diagonal_upper(jax.random.fold_in(splits[8], 71), 0)
    parents_lower = draw_parents_lower(jax.random.fold_in(splits[8], 71), 0)
    blocks_lower = draw_blocks_lower(jax.random.fold_in(splits[8], 71), 0)
    factor_lower = normal_values(splits[6], (LOWER, 2, CS, W), (2 * CS) ** -0.5, 0.1875, ((2, 16), (3, 2)), jnp.float32)
    diagonal_lower = draw_diagonal_lower(jax.random.fold_in(splits[8], 71), 0)
    return {"top_inverse": top_inverse, "blocks_upper": blocks_upper, "factor_upper": factor_upper, "diagonal_upper": diagonal_upper, "parents_lower": parents_lower, "blocks_lower": blocks_lower, "factor_lower": factor_lower, "diagonal_lower": diagonal_lower}


def complex_dot(left_side, right_side):
    highest = lax.Precision.HIGHEST

    def real_dot(first_matrix, second_matrix):
        return jnp.dot(first_matrix, second_matrix, precision=highest, preferred_element_type=jnp.float32)

    real_part = real_dot(left_side[0], right_side[0]) - real_dot(left_side[1], right_side[1])
    imag_part = real_dot(left_side[0], right_side[1]) + real_dot(left_side[1], right_side[0])
    return jnp.stack([real_part, imag_part])


def transpose_pair(matrix):
    return jnp.swapaxes(matrix, 1, 2)


def restrict(matrix, blocks, blocks_total):
    tiled_view = matrix.reshape(2, BS, blocks_total, BS, blocks_total)
    tiled_view = jnp.take(tiled_view, blocks, axis=2)
    tiled_view = jnp.take(tiled_view, blocks, axis=4)
    return tiled_view.reshape(2, BS * NB, BS * NB)


def supernode(ancestors, factor, diagonal):
    coupled = -complex_dot(ancestors, factor)
    block_inverse = diagonal - complex_dot(transpose_pair(factor), coupled)
    return transpose_pair(coupled), block_inverse


def reference(top_inverse, blocks_upper, factor_upper, diagonal_upper, parents_lower, blocks_lower, factor_lower, diagonal_lower):
    upper_coupling = []
    upper_blocks = []
    for sibling in range(UPPER):
        ancestors = restrict(top_inverse, blocks_upper[sibling], NTB)
        coupling_out, block_out = supernode(ancestors, factor_upper[sibling], diagonal_upper[sibling])
        upper_coupling.append(coupling_out)
        upper_blocks.append(block_out)
    coupling_inverse_upper = jnp.stack(upper_coupling)
    block_inverse_upper = jnp.stack(upper_blocks)
    lower_coupling = []
    lower_blocks = []
    for grandchild in range(LOWER):
        source = jnp.take(block_inverse_upper, parents_lower[grandchild], axis=0)
        ancestors = restrict(source, blocks_lower[grandchild], KB)
        coupling_out, block_out = supernode(ancestors, factor_lower[grandchild], diagonal_lower[grandchild])
        lower_coupling.append(coupling_out)
        lower_blocks.append(block_out)
    coupling_inverse_lower = jnp.stack(lower_coupling)
    block_inverse_lower = jnp.stack(lower_blocks)
    return (coupling_inverse_upper, block_inverse_upper, coupling_inverse_lower, block_inverse_lower)
```

```python
import jax
import jax.numpy as jnp
from jax import lax
from jax.sharding import PartitionSpec as P

HIGH = lax.Precision.HIGH
EXACT = lax.Precision.HIGHEST


def one_hot_rows(blocks, blocks_total, inner):
    chosen_blocks = blocks.shape[1]
    rows = lax.broadcasted_iota(jnp.int32, (inner * chosen_blocks, inner * blocks_total), 0)
    cols = lax.broadcasted_iota(jnp.int32, (inner * chosen_blocks, inner * blocks_total), 1)
    same = rows // chosen_blocks == cols // blocks_total
    wanted = jnp.zeros((blocks.shape[0],) + rows.shape, jnp.int32)
    for b in range(chosen_blocks):
        wanted = jnp.where(rows % chosen_blocks == b, blocks[:, b, None, None], wanted)
    return jnp.where(same & (cols % blocks_total == wanted), 1.0, 0.0).astype(jnp.float32)


def complex_product(first_side, second_side, pattern, precision):
    def part(i, j):
        return jnp.einsum(
            pattern,
            first_side[:, i],
            second_side[:, j],
            precision=precision,
            preferred_element_type=jnp.float32,
        )

    return jnp.stack([part(0, 0) - part(1, 1), part(0, 1) + part(1, 0)], axis=1)


def restrict(source, blocks, blocks_total):
    rows_within = source.shape[2] // blocks_total
    cols_within = source.shape[3] // blocks_total
    rows = one_hot_rows(blocks, blocks_total, rows_within)
    cols = one_hot_rows(blocks, blocks_total, cols_within)
    picked = jnp.einsum("bmk,bikn->bimn", rows, source, precision=EXACT)
    return jnp.einsum("bimn,bjn->bimj", picked, cols, precision=EXACT)


def my_columns(factor_columns, root_col):
    mine = lax.axis_index("col") == root_col
    return lax.psum(jnp.where(mine, factor_columns, jnp.zeros_like(factor_columns)), "col")


def supernodes(ancestors, mine, gathered, diagonal):
    coupled = -complex_product(mine, ancestors, "bkm,bkn->bmn", HIGH)
    coupled = lax.all_gather(coupled, "col", axis=3, tiled=True)
    return coupled, diagonal - complex_product(coupled, gathered, "bmk,bkn->bmn", HIGH)


def shards(
    top_inverse,
    blocks_upper,
    factor_upper,
    diagonal_upper,
    parents_lower,
    blocks_lower,
    factor_lower,
    diagonal_lower,
):
    row_devices = lax.axis_size("row")
    ratio = row_devices // lax.axis_size("col")
    rows_here = diagonal_upper.shape[2]
    my_row = lax.axis_index("row")
    root_col = my_row // ratio
    slice_start = my_row % ratio * rows_here
    across = factor_upper.shape[2] * row_devices
    kb = rows_here * row_devices // (across // blocks_upper.shape[1])
    ntb = top_inverse.shape[1] * row_devices // (across // blocks_upper.shape[1])

    source = jnp.broadcast_to(top_inverse, (blocks_upper.shape[0],) + top_inverse.shape)
    picked = restrict(source, blocks_upper, ntb)
    ancestors = lax.all_gather(picked, "row", axis=2, tiled=True)
    gathered_upper = lax.all_gather(factor_upper, "row", axis=2, tiled=True)
    gathered_lower = lax.all_gather(factor_lower, "row", axis=2, tiled=True)
    mine = my_columns(lax.dynamic_slice_in_dim(gathered_upper, slice_start, rows_here, 3), root_col)
    upper_coupling, upper_blocks = supernodes(ancestors, mine, gathered_upper, diagonal_upper)

    source = jnp.take(upper_blocks, parents_lower, axis=0)
    picked = restrict(source, blocks_lower, kb)
    ancestors = lax.all_gather(picked, "row", axis=2, tiled=True)
    mine = my_columns(lax.dynamic_slice_in_dim(gathered_lower, slice_start, rows_here, 3), root_col)
    lower_coupling, lower_blocks = supernodes(ancestors, mine, gathered_lower, diagonal_lower)
    return upper_coupling, upper_blocks, lower_coupling, lower_blocks


def solution(mesh):
    split = P(None, None, "row", "col")
    return jax.shard_map(
        shards,
        mesh=mesh,
        in_specs=(P(None, "row", "col"), P(), split, split, P(), P(), split, split),
        out_specs=(P(None, None, "row", None), split, P(None, None, "row", None), split),
        check_vma=False,
    )
```

```python
import jax
import jax.numpy as jnp
from jax import lax
from jax.experimental import pallas as pl
from jax.experimental.pallas import tpu as pltpu
from jax.sharding import PartitionSpec as P

BS = 256
KB = 16
NB = 2
NTB = 4
UPPER = 2


def from_root(block, axis, source):
    block = jnp.where(lax.axis_index(axis) == source, block, jnp.zeros_like(block))
    return lax.psum(block, axis)


def complex_product(first_side, second_side, pattern):
    pieces_all = jnp.einsum(
        pattern,
        first_side,
        second_side,
        precision=lax.Precision.HIGHEST,
        preferred_element_type=jnp.float32,
    )
    real_part = pieces_all[:, 0, 0] - pieces_all[:, 1, 1]
    imag_part = pieces_all[:, 0, 1] + pieces_all[:, 1, 0]
    return jnp.stack([real_part, imag_part], axis=1)


def pick_blocks(stacked, blocks, blocks_total, rows_within, cols_within):
    batch_size = stacked.shape[0]
    tiled_view = stacked.reshape(
        batch_size, 2, rows_within, blocks_total, cols_within, blocks_total
    )

    def pick_single(matrix, chosen):
        matrix = jnp.take(matrix, chosen, axis=2)
        matrix = jnp.take(matrix, chosen, axis=4)
        return matrix.reshape(2, rows_within * NB, cols_within * NB)

    return jax.vmap(pick_single)(tiled_view, blocks)


def supernode_level(chosen, factor_rows, diag_block, slice_start, root_col):
    gathered_factor = lax.all_gather(factor_rows, "row", axis=2, tiled=True)
    factor_columns = lax.dynamic_slice_in_dim(gathered_factor, slice_start, diag_block.shape[2], 3)
    factor_slice = from_root(factor_columns, "col", root_col)
    zeroes = jnp.zeros(
        factor_slice.shape[:2] + (factor_slice.shape[3], chosen.shape[3]), jnp.float32
    )
    factor_part = factor_slice
    coupled_part = zeroes - complex_product(
        factor_part, lax.all_gather(chosen, "row", axis=2, tiled=True), "bikm,bjkn->bijmn"
    )
    incoming = lax.all_gather(coupled_part, "col", axis=3, tiled=True)
    block_total = diag_block
    factor_part = gathered_factor
    block_total = block_total - complex_product(incoming, factor_part, "bimk,bjkn->bijmn")
    gathered = incoming
    block_total, gathered = (block_total, gathered)
    return (gathered, block_total)


def shards(
    top_inverse,
    blocks_upper,
    factor_upper,
    diagonal_upper,
    parents_lower,
    blocks_lower,
    factor_lower,
    diagonal_lower,
):
    row_devices = lax.axis_size("row")
    col_devices = lax.axis_size("col")
    rows_within = BS // row_devices
    cols_within = BS // col_devices
    ratio_axes = row_devices // col_devices
    my_row = lax.axis_index("row")
    root_col = my_row // ratio_axes
    slice_start = my_row % ratio_axes * rows_within * KB
    upper_spans = (0, UPPER)
    first_index, last_index = upper_spans
    width_now = last_index - first_index
    source = jnp.broadcast_to(top_inverse, (width_now,) + top_inverse.shape)
    chosen = pick_blocks(source, blocks_upper, NTB, rows_within, cols_within)
    coupling_out, block_out = supernode_level(
        chosen, factor_upper, diagonal_upper, slice_start, root_col
    )
    upper_coupling = coupling_out
    upper_blocks = block_out
    source = jnp.take(upper_blocks, parents_lower, axis=0)
    chosen = pick_blocks(source, blocks_lower, KB, rows_within, cols_within)
    coupling_out, block_out = supernode_level(
        chosen, factor_lower, diagonal_lower, slice_start, root_col
    )
    return (upper_coupling, upper_blocks, coupling_out, block_out)


NZ, NY, NX = 4, 2, 2
TILE = 256
ROUTES = (("zyx", 0, 640), ("zxy", 640, 640), ("xzy", 1280, 384), ("yzx", 1664, 384))
SMALL = (("zyx", 0, 128), ("zxy", 128, 128))
EXACT = lax.Precision.HIGHEST


def split(value):
    high = value.astype(jnp.bfloat16)
    return high, (value - high.astype(jnp.float32)).astype(jnp.bfloat16)


def dot(a, b):
    return jnp.dot(a, b, preferred_element_type=jnp.float32)


def dot3(a, b):
    return dot(a[0], b[0]) + (dot(a[0], b[1]) + dot(a[1], b[0]))


def fused(
    fu, fl, au, du, dl, pick, ends,
    ct_out, b_out, gathered,
    anc, mine, ct, left, gbuf, dbuf, obuf, picked,
    fsend, frecv, asend, arecv, msend, mrecv, mlocal, csend, crecv, own_sem, tile_in, tile_out, ct_sem,
):
    row, col = lax.axis_index("row"), lax.axis_index("col")
    z, y, x = row // (NY * NX), row // NX % NY, row % NX
    root = row // 8
    place = {"z": z, "y": y, "x": x}
    size = {"z": NZ, "y": NY, "x": NX}

    def device(dim, step):
        at = dict(place)
        at[dim] = lax.rem(at[dim] + step, size[dim])
        return (at["z"] * (NY * NX) + at["y"] * NX + at["x"], col)

    other = (row, 1 - col)
    barrier = pltpu.get_barrier_semaphore()
    peers = [device("z", 1), device("z", 2), device("z", 3), device("y", 1), device("x", 1), other]
    for peer in peers:
        pl.semaphore_signal(barrier, inc=1, device_id=peer, device_id_type=pl.DeviceIdType.MESH)
    pl.semaphore_wait(barrier, len(peers))

    def region(buf, number, full, cols):
        at = [slice(None) if d in full else pl.ds(place[d], 1) for d in "zyx"]
        return buf.at[pl.ds(2 * number, 2), at[0], at[1], at[2], :, cols]

    def messages(buf, routes, send, recv, number, phase):
        made = []
        for r, (order, first, width) in enumerate(routes):
            dim = order[phase]
            ref = region(buf, number, order[:phase], pl.ds(first, width))
            for step in range(1, size[dim]):
                sem = (number, r, {"z": 0, "y": 3, "x": 4}[dim] + step - 1)
                made.append(
                    pltpu.make_async_remote_copy(
                        src_ref=ref,
                        dst_ref=ref,
                        send_sem=send.at[sem],
                        recv_sem=recv.at[sem],
                        device_id=device(dim, step),
                        device_id_type=pl.DeviceIdType.MESH,
                    )
                )
        return made

    pending = []

    def start(made):
        for m in made:
            m.start()
        pending.extend(made)

    def arrive(made):
        for m in made:
            m.wait_recv()

    def f_msg(number, phase):
        return messages(gathered, ROUTES, fsend, frecv, number, phase)

    def a_msg(numbers, phase):
        made = []
        for number in numbers:
            made += messages(anc, SMALL, asend, arecv, number, phase)
        return made

    upper, lower = fu.shape[0] // 2, fl.shape[0] // 2
    total = upper + lower
    ups, lows = range(upper), range(upper, total)
    whole = pl.ds(0, fu.shape[5])

    locals_ = []
    for s in range(total):
        src = fu.at[pl.ds(2 * s, 2)] if s < upper else fl.at[pl.ds(2 * (s - upper), 2)]
        locals_.append(pltpu.make_async_copy(src, region(gathered, s, "", whole), own_sem.at[s]))
    for s in ups:
        locals_.append(pltpu.make_async_copy(au.at[pl.ds(2 * s, 2)], region(anc, s, "", pl.ds(0, 256)), own_sem.at[total + s]))
    for c in locals_:
        c.start()
    for c in locals_:
        c.wait()

    def move_mine(s):
        columns = pl.ds(pl.multiple_of(lax.rem(row, 8) * TILE, TILE), TILE)
        src = gathered.at[pl.ds(2 * s, 2), :, :, :, :, columns]
        remote = pltpu.make_async_remote_copy(
            src_ref=src, dst_ref=mine.at[s], send_sem=msend.at[s], recv_sem=mrecv.at[s],
            device_id=other, device_id_type=pl.DeviceIdType.MESH,
        )

        @pl.when(col == root)
        def _():
            remote.start()
            here = pltpu.make_async_copy(src, mine.at[s], mlocal.at[s])
            here.start()
            here.wait()
            remote.wait_send()

        @pl.when(col != root)
        def _():
            remote.wait_recv()

    def compute(s):
        is_upper = s < upper
        diag = du if is_upper else dl
        d_at = s if is_upper else s - upper
        move_mine(s)
        turned = split(mine[s].reshape(1024, TILE).T)
        a_all = anc[2 * s : 2 * s + 2].reshape(2, 512, TILE)
        ar, ai = a_all[0], a_all[1]
        right = jnp.concatenate(
            [jnp.concatenate([-ar, -ai], axis=1), jnp.concatenate([ai, -ar], axis=1)], axis=0
        )
        half = dot3(turned, split(right))
        cols = pl.ds(pl.multiple_of(col * TILE, TILE), TILE)
        ct[s, 0, :, cols] = half[:, :TILE]
        ct[s, 1, :, cols] = half[:, TILE:]
        swap = pltpu.make_async_remote_copy(
            src_ref=ct.at[s, :, :, cols], dst_ref=ct.at[s, :, :, cols],
            send_sem=csend.at[s], recv_sem=crecv.at[s],
            device_id=other, device_id_type=pl.DeviceIdType.MESH,
        )
        swap.start()
        swap.wait()
        out = pltpu.make_async_copy(ct.at[s], ct_out.at[s], ct_sem)
        out.start()
        cr, ci = split(ct[s, 0]), split(ct[s, 1])
        for k in range(2):
            left[k, :TILE, :512] = cr[k]
            left[k, :TILE, 512:] = -ci[k]
            left[k, TILE:, :512] = ci[k]
            left[k, TILE:, 512:] = cr[k]

        tiles = fu.shape[5] // TILE

        def span(n):
            return pl.ds(n * TILE if isinstance(n, int) else pl.multiple_of(n * TILE, TILE), TILE)

        def loads(n, slot):
            return (
                pltpu.make_async_copy(gathered.at[pl.ds(2 * s, 2), :, :, :, :, span(n)], gbuf.at[slot], tile_in.at[0, slot]),
                pltpu.make_async_copy(diag.at[d_at, :, :, span(n)], dbuf.at[slot], tile_in.at[1, slot]),
            )

        def store(n, slot):
            return pltpu.make_async_copy(obuf.at[slot], b_out.at[s, :, :, span(n)], tile_out.at[slot])

        for c in loads(0, 0):
            c.start()

        @pl.loop(0, tiles)
        def _(n):
            slot = lax.rem(n, 2)

            @pl.when(n + 1 < tiles)
            def _():
                for c in loads(n + 1, 1 - slot):
                    c.start()

            for c in loads(n, slot):
                c.wait()

            @pl.when(n >= 2)
            def _():
                store(n - 2, slot).wait()

            rows = split(gbuf[slot].reshape(1024, TILE))
            block = dbuf[slot].reshape(512, TILE) - dot3((left[0], left[1]), rows)
            obuf[slot] = block.reshape(2, TILE, TILE)
            store(n, slot).start()
            if is_upper:
                for k in range(2):
                    parts = split(block[k * TILE : (k + 1) * TILE])
                    chosen = dot(pick[s], parts[0]) + dot(pick[s], parts[1])
                    if s == 0:
                        picked[k, :, span(n)] = chosen
                    else:
                        picked[k, :, span(n)] += chosen

        store(tiles - 2, 0).wait()
        store(tiles - 1, 1).wait()
        out.wait()

    def pick_lower():
        for t in range(lower):
            for k in range(2):
                for h in range(2):
                    rows = split(picked[k, 32 * t : 32 * t + 32, 1024 * h : 1024 * h + 1024])
                    value = dot(rows[0], ends[t]) + dot(rows[1], ends[t])
                    anc[2 * (upper + t) + k, z, y, x, :, 128 * h : 128 * h + 128] = value

    start(a_msg(ups, 0))
    start(f_msg(0, 0))
    start(f_msg(1, 0))
    arrive(a_msg(ups, 0))
    start(a_msg(ups, 1))
    arrive(f_msg(0, 0))
    start(f_msg(0, 1))
    start(f_msg(2, 0))
    arrive(a_msg(ups, 1))
    start(a_msg(ups, 2))
    arrive(f_msg(1, 0))
    start(f_msg(1, 1))
    arrive(f_msg(0, 1))
    start(f_msg(0, 2))
    start(f_msg(3, 0))
    arrive(f_msg(2, 0))
    start(f_msg(2, 1))
    arrive(f_msg(1, 1))
    start(f_msg(1, 2))
    start(f_msg(4, 0))
    arrive(a_msg(ups, 2))
    arrive(f_msg(0, 2))
    compute(0)
    arrive(f_msg(3, 0))
    start(f_msg(3, 1))
    arrive(f_msg(1, 2))
    compute(1)
    pick_lower()
    start(a_msg(lows, 0))
    arrive(f_msg(2, 1))
    start(f_msg(2, 2))
    arrive(f_msg(4, 0))
    start(f_msg(4, 1))
    arrive(a_msg(lows, 0))
    start(a_msg(lows, 1))
    arrive(f_msg(3, 1))
    start(f_msg(3, 2))
    arrive(a_msg(lows, 1))
    start(a_msg(lows, 2))
    arrive(f_msg(4, 1))
    start(f_msg(4, 2))
    arrive(a_msg(lows, 2))
    arrive(f_msg(2, 2))
    compute(2)
    arrive(f_msg(3, 2))
    compute(3)
    arrive(f_msg(4, 2))
    compute(4)
    for m in pending:
        m.wait_send()


def one_hot_rows(blocks, blocks_total, inner):
    chosen_blocks = blocks.shape[1]
    shape = (inner * chosen_blocks, inner * blocks_total)
    rows = lax.broadcasted_iota(jnp.int32, shape, 0)
    cols = lax.broadcasted_iota(jnp.int32, shape, 1)
    wanted = jnp.zeros((blocks.shape[0],) + shape, jnp.int32)
    for b in range(chosen_blocks):
        wanted = jnp.where(rows % chosen_blocks == b, blocks[:, b, None, None], wanted)
    same = rows // chosen_blocks == cols // blocks_total
    return jnp.where(same & (cols % blocks_total == wanted), 1.0, 0.0).astype(jnp.float32)


def fused_shards(top_inverse, blocks_upper, factor_upper, diagonal_upper, parents_lower, blocks_lower, factor_lower, diagonal_lower):
    upper, lower = factor_upper.shape[0], factor_lower.shape[0]
    total = upper + lower
    width = factor_upper.shape[3]
    rows = one_hot_rows(blocks_upper, NTB, top_inverse.shape[1] // NTB)
    cols = one_hot_rows(blocks_upper, NTB, top_inverse.shape[2] // NTB)
    au = jnp.einsum("bmk,ikn->bimn", rows, top_inverse, precision=EXACT)
    au = jnp.einsum("bimn,bjn->bimj", au, cols, precision=EXACT)
    rows = one_hot_rows(blocks_lower, KB, 16)
    mine = (parents_lower[None, :] == jnp.arange(upper)[:, None]).astype(jnp.float32)
    pick = (mine[:, :, None, None] * rows[None]).reshape(upper, lower * 32, 256).astype(jnp.bfloat16)
    ends = jnp.swapaxes(one_hot_rows(blocks_lower, KB, 64), 1, 2).astype(jnp.bfloat16)

    def cut(value):
        return value.reshape(-1, 1, 1, 1, 32, value.shape[-1])

    spec = pl.BlockSpec(memory_space=pl.ANY)
    inside = pl.BlockSpec(memory_space=pltpu.VMEM)
    f32, bf16 = jnp.float32, jnp.bfloat16
    dma = pltpu.SemaphoreType.DMA
    ct, block, _ = pl.pallas_call(
        fused,
        out_shape=(
            jax.ShapeDtypeStruct((total, 2, 256, 512), f32),
            jax.ShapeDtypeStruct((total, 2, 256, width), f32),
            jax.ShapeDtypeStruct((2 * total, NZ, NY, NX, 32, width), f32),
        ),
        in_specs=[spec] * 5 + [inside] * 2,
        out_specs=(spec,) * 3,
        scratch_shapes=[
            pltpu.VMEM((2 * total, NZ, NY, NX, 32, TILE), f32),
            pltpu.VMEM((total, 2, NZ, NY, NX, 32, TILE), f32),
            pltpu.VMEM((total, 2, 256, 512), f32),
            pltpu.VMEM((2, 512, 1024), bf16),
            pltpu.VMEM((2, 2, NZ, NY, NX, 32, TILE), f32),
            pltpu.VMEM((2, 2, TILE, TILE), f32),
            pltpu.VMEM((2, 2, TILE, TILE), f32),
            pltpu.VMEM((2, lower * 32, width), f32),
            dma((total, 4, 5)),
            dma((total, 4, 5)),
            dma((total, 2, 5)),
            dma((total, 2, 5)),
            dma((total,)),
            dma((total,)),
            dma((total,)),
            dma((total,)),
            dma((total,)),
            dma((total + upper,)),
            dma((2, 2)),
            dma((2,)),
            dma,
        ],
        compiler_params=pltpu.CompilerParams(
            collective_id=0, has_side_effects=True, vmem_limit_bytes=52 * 1024 * 1024
        ),
    )(cut(factor_upper), cut(factor_lower), cut(au), diagonal_upper, diagonal_lower, pick, ends)
    return ct[:upper], block[:upper], ct[upper:], block[upper:]


def solution(mesh):
    placed = (
        P(None, "row", "col"),
        P(),
        P(None, None, "row", "col"),
        P(None, None, "row", "col"),
        P(),
        P(),
        P(None, None, "row", "col"),
        P(None, None, "row", "col"),
    )
    fits = dict(mesh.shape) == {"row": NZ * NY * NX, "col": 2}
    return jax.shard_map(
        fused_shards if fits else shards,
        mesh=mesh,
        in_specs=placed,
        out_specs=(
            P(None, None, "row", None),
            P(None, None, "row", "col"),
            P(None, None, "row", None),
            P(None, None, "row", "col"),
        ),
        check_vma=False,
    )
```
